32 devices in a mesh: modes: 4 (over y, core), sites: 8 (over z, x).
Axes of the slice: x: 2, y: 2, z: 4, core: 2. Of those that a mesh axis runs over, the one named last changes fastest.
Arguments:
- eigvecs: bfloat16 [2, 2048, 12, 4096], P(None, 'modes', None, 'sites'), may hold values from -6 to 6
- eigenvalues: float32 [2048], P('modes'), may hold values from -64 to 64, as said below
- source_sites: int32 [2], replicated, may hold values from 0 to 4095
Outputs:
- propagator: float32 [24, 2, 12, 4096], P('modes', None, None, 'sites')
The draws below stay inside these ranges and needn't reach their ends.
Inputs may be any that keep to these rules, and one draw needn't show every extreme that they name: `eigenvalues`: magnitudes between 8 and 64, of either sign.
All inputs are finite; a program needn't handle non-finite values.
Results may differ from the reference program's by a relative error of at most 0.0029.
Values may be sent and summed in bfloat16 or wider, within the bound.
No kernel may reach another device: no remote copies, remote signals or barrier semaphores. Data moves between devices by JAX's collectives and lax.ppermute only.
A program may use at most 128 MiB of HBM per device.

```python
import math
import jax
import jax.numpy as jnp
from jax import lax

MODES = 2048
SC = 12
NSRC = 2
NS = 4096


def draw_eigenvalues(key, part):
    key = jax.random.fold_in(key, 7)
    first_key, second_key = jax.random.split(key)
    magnitude = jnp.exp(jax.random.uniform(first_key, (MODES,), jnp.float32, math.log(8.0), math.log(64.0)))
    signs = jax.random.randint(second_key, (MODES,), 0, 2).astype(jnp.float32) * 2.0 - 1.0
    return magnitude * signs


def shard_levels(own_key, shape, pieces, least, high):
    level = 1.0
    for axis_at, blocks in pieces:
        steps = jax.random.uniform(jax.random.fold_in(jax.random.fold_in(own_key, 6), axis_at), (blocks,), jnp.float32, least / len(pieces), high / len(pieces))
        level = level * jnp.repeat(jnp.exp(steps), shape[axis_at] // blocks).reshape((-1,) + (1,) * (len(shape) - 1 - axis_at))
    return level


def scatter_about(stream_key, extent, width, bound, cuts=(), kind=jnp.bfloat16):
    array = width * jax.random.normal(stream_key, extent, jnp.float32)
    if cuts:
        array = array * shard_levels(stream_key, extent, cuts, -0.22, 0.18)
    return jnp.clip(array, -bound, bound).astype(kind)


def setup_inputs(seed: int = 0) -> dict:
    seeds = jax.random.split(jax.random.key(seed), 4)
    eigvecs = scatter_about(seeds[0], (2, MODES, SC, NS), 1.0, 6.0, ((1, 4), (3, 8)))
    eigenvalues = draw_eigenvalues(jax.random.fold_in(seeds[3], 71), 0)
    source_sites = jax.random.randint(seeds[2], (NSRC,), 0, NS).astype(jnp.int32)
    return dict(eigvecs=eigvecs, eigenvalues=eigenvalues, source_sites=source_sites)


def reference(eigvecs, eigenvalues, source_sites):
    picked = jnp.take(eigvecs, source_sites, axis=3)
    source_rows = jnp.transpose(picked, (0, 1, 3, 2)).reshape(2, MODES, NSRC * SC)
    divisor = eigenvalues[:, None]
    weight_real = (source_rows[0].astype(jnp.float32) / divisor).astype(jnp.bfloat16)
    weight_imag = (-source_rows[1].astype(jnp.float32) / divisor).astype(jnp.bfloat16)
    column_real = jnp.concatenate([weight_real, -weight_imag], axis=0)
    column_imag = jnp.concatenate([weight_imag, weight_real], axis=0)
    weights = jnp.stack([column_real, column_imag], axis=2).reshape(2 * MODES, 2 * NSRC * SC)
    transposed = weights.T

    def one_component(component):
        sliced = lax.dynamic_index_in_dim(eigvecs, component, 2, keepdims=False)
        flattened = sliced.reshape(2 * MODES, NS)
        return jnp.dot(transposed, flattened, preferred_element_type=jnp.float32)

    stacked = lax.map(one_component, jnp.arange(SC, dtype=jnp.int32))
    result = jnp.transpose(stacked, (1, 0, 2)).reshape(NSRC * SC, 2, SC, NS)
    return result
```

```python
import functools
import jax
import jax.numpy as jnp
from jax import lax
from jax.experimental import pallas as pl
from jax.experimental.pallas import tpu as pltpu
from jax.sharding import PartitionSpec as P

LANES = 128
MIB = 2**20


def pick_kernel(sites_ref, vectors_ref, rows_ref, columns_ref, total_ref, sems):
    parts, spin_color, mode_count, site_count = vectors_ref.shape
    source_count = sites_ref.shape[0]
    columns = source_count * spin_color
    first = lax.axis_index("sites") * site_count
    local = [sites_ref[number] - first for number in range(source_count)]
    held = [(index >= 0) & (index < site_count) for index in local]

    def copy(number, part):
        start = pl.multiple_of(local[number] // LANES * LANES, LANES)
        return pltpu.make_async_copy(
            vectors_ref.at[part, :, :, pl.ds(start, LANES)],
            columns_ref.at[number, part],
            sems.at[number, part],
        )

    for number in range(source_count):
        @pl.when(held[number])
        def _(number=number):
            for part in range(parts):
                copy(number, part).start()

    total_ref[...] = jnp.zeros_like(total_ref)
    row = lax.broadcasted_iota(jnp.int32, (columns, LANES), 0)
    lane = lax.broadcasted_iota(jnp.int32, (columns, LANES), 1)
    for number in range(source_count):
        @pl.when(held[number])
        def _(number=number):
            for part in range(parts):
                copy(number, part).wait()
                total = jnp.zeros((columns, mode_count), jnp.float32)
                for component in range(spin_color):
                    chosen = (row == number * spin_color + component) & (lane == local[number] % LANES)
                    total += lax.dot_general(
                        jnp.where(chosen, 1.0, 0.0).astype(jnp.bfloat16),
                        columns_ref[number, part, component],
                        (((1,), (1,)), ((), ())),
                        preferred_element_type=jnp.float32,
                    )
                total_ref[pl.ds(part * columns, columns), :] += total
    rows_ref[...] = total_ref[...].astype(rows_ref.dtype)


def pick(source_sites, vectors):
    parts, spin_color, mode_count, site_count = vectors.shape
    source_count = source_sites.shape[0]
    rows = parts * source_count * spin_color
    return pl.pallas_call(
        pick_kernel,
        out_shape=jax.ShapeDtypeStruct((rows, mode_count), vectors.dtype),
        in_specs=[pl.BlockSpec(memory_space=pltpu.SMEM), pl.BlockSpec(memory_space=pl.ANY)],
        out_specs=pl.BlockSpec(memory_space=pltpu.VMEM),
        scratch_shapes=[
            pltpu.VMEM((source_count, parts, spin_color, mode_count, LANES), vectors.dtype),
            pltpu.VMEM((rows, mode_count), jnp.float32),
            pltpu.SemaphoreType.DMA((source_count, parts)),
        ],
        compiler_params=pltpu.CompilerParams(vmem_limit_bytes=16 * MIB),
        name="pick",
    )(source_sites, vectors)


def iota(shape, dim):
    return lax.broadcasted_iota(jnp.int32, shape, dim)


def shares(columns, ways, core, plane):
    share = columns // ways
    shape = (2 * columns, 2 * columns)
    row, entry = iota(shape, 0), iota(shape, 1)
    place, inner = row // (2 * share), row % (2 * share)
    its_core = jnp.where(place < 2, 1 - core, core)
    its_plane = jnp.where((place == 0) | (place == 3), plane, 1 - plane)
    column, part = (2 * its_plane + its_core) * share + inner // 2, inner % 2
    real, imag = (entry == column), (entry == column + columns)
    one = jnp.float32(1)
    zero = jnp.float32(0)
    on_real = jnp.where(part == 0, jnp.where(real, one, zero), jnp.where(imag, one, zero))
    on_imag = jnp.where(part == 0, jnp.where(imag, -one, zero), jnp.where(real, one, zero))
    return on_real.astype(jnp.bfloat16), on_imag.astype(jnp.bfloat16)


def dot(left, right):
    return jnp.dot(left, right, preferred_element_type=jnp.float32)


def project_kernel(rows_ref, values_ref, vectors_ref, sent_ref, kept_ref, flat_ref):
    parts, spin_color, mode_count, site_count = vectors_ref.shape
    columns = rows_ref.shape[0] // 2
    ways = 4
    share = 2 * columns // ways
    index = lax.axis_index("modes")
    divisor = values_ref[...]
    real = rows_ref[:columns, :].astype(jnp.float32) / divisor
    imag = -rows_ref[columns:, :].astype(jnp.float32) / divisor
    weights = jnp.concatenate([real, imag], axis=0).astype(jnp.bfloat16)
    on_real, on_imag = shares(columns, ways, index % 2, index // 2)
    left_real = dot(on_real, weights).astype(jnp.bfloat16)
    left_imag = dot(on_imag, weights).astype(jnp.bfloat16)
    for component in range(spin_color):
        product = dot(left_real, vectors_ref[0, component]) + dot(left_imag, vectors_ref[1, component])
        for place in range(ways):
            flat_ref[place, pl.ds(component * share, share), :] = product[place * share:(place + 1) * share]
    sent_ref[...] = flat_ref[:2].astype(sent_ref.dtype)
    kept_ref[...] = flat_ref[2:].astype(kept_ref.dtype)


def project(rows, eigenvalues, vectors):
    parts, spin_color, mode_count, site_count = vectors.shape
    share = rows.shape[0] // 4 * spin_color
    shape = (2, share, site_count)
    return pl.pallas_call(
        project_kernel,
        out_shape=[jax.ShapeDtypeStruct(shape, jnp.bfloat16), jax.ShapeDtypeStruct(shape, jnp.float32)],
        in_specs=[pl.BlockSpec(memory_space=pltpu.VMEM)] * 3,
        out_specs=[pl.BlockSpec(memory_space=pltpu.VMEM)] * 2,
        scratch_shapes=[pltpu.VMEM((4, share, site_count), jnp.float32)],
        compiler_params=pltpu.CompilerParams(vmem_limit_bytes=32 * MIB),
        name="project",
    )(rows, eigenvalues.reshape(1, mode_count), vectors)


def swap(block, axis, size, bit):
    return lax.ppermute(block, axis, [(index, index ^ bit) for index in range(size)])


def on_device(eigvecs, eigenvalues, source_sites):
    site_ways, mode_ways = lax.axis_size("sites"), lax.axis_size("modes")
    vectors = jnp.transpose(eigvecs, (0, 2, 1, 3))
    parts, spin_color, mode_count, site_count = vectors.shape
    rows = pick(source_sites, vectors)
    bit = 1
    while bit < site_ways:
        rows = rows + swap(rows, "sites", site_ways, bit)
        bit *= 2
    sent, kept = project(rows, eigenvalues, vectors)
    got = swap(sent, "modes", mode_ways, 1)
    across = (kept[0] + got[1].astype(jnp.float32)).astype(jnp.bfloat16)
    arrived = swap(across, "modes", mode_ways, 2)
    total = kept[1] + got[0].astype(jnp.float32) + arrived.astype(jnp.float32)
    share = total.shape[0] // spin_color // 2
    return jnp.transpose(total.reshape(spin_color, share, 2, site_count), (1, 2, 0, 3))


def solution(mesh):
    in_specs = (P(None, "modes", None, "sites"), P("modes"), P())
    out_specs = P("modes", None, None, "sites")
    return jax.shard_map(on_device, mesh=mesh, in_specs=in_specs, out_specs=out_specs, check_vma=False)
```

```python
import jax
import jax.numpy as jnp
from jax import lax
from jax.experimental import pallas as pl
from jax.experimental.pallas import tpu as pltpu
from jax.sharding import PartitionSpec as P

LANES = 128
MIB = 2**20
GROUPS = [[1, 2, 3], [4]]


def pick_kernel(given_ref, vectors_ref, rows_ref, sites_ref, columns_ref, total_ref, given_sem, sems):
    given = pltpu.make_async_copy(given_ref, sites_ref, given_sem)
    given.start()
    total_ref[...] = jnp.zeros_like(total_ref)
    given.wait()
    parts, spin_color, mode_count, site_count = vectors_ref.shape
    source_count = sites_ref.shape[0]
    first = lax.axis_index("sites") * site_count
    local = [sites_ref[number] - first for number in range(source_count)]
    held = [(index >= 0) & (index < site_count) for index in local]

    def copy(number, part):
        start = pl.multiple_of(local[number] // LANES * LANES, LANES)
        return pltpu.make_async_copy(
            vectors_ref.at[part, :, :, pl.ds(start, LANES)],
            columns_ref.at[number, part],
            sems.at[number, part],
        )

    for number in range(source_count):
        @pl.when(held[number])
        def _(number=number):
            for part in range(parts):
                copy(number, part).start()

    lane = lax.broadcasted_iota(jnp.int32, (8, LANES), 1)
    for number in range(source_count):
        @pl.when(held[number])
        def _(number=number):
            chosen = jnp.where(lane == local[number] % LANES, 1.0, 0.0).astype(jnp.bfloat16)
            for part in range(parts):
                copy(number, part).wait()
                row = lax.dot_general(
                    chosen,
                    columns_ref[number, part].reshape(spin_color * mode_count, LANES),
                    (((1,), (1,)), ((), ())),
                    preferred_element_type=jnp.float32,
                )
                base = (part * source_count + number) * spin_color
                for component in range(spin_color):
                    total_ref[base + component, :] = row[0, component * mode_count:(component + 1) * mode_count]
    rows_ref[...] = total_ref[...].astype(rows_ref.dtype)


def pick(source_sites, vectors):
    parts, spin_color, mode_count, site_count = vectors.shape
    source_count = source_sites.shape[0]
    rows = parts * source_count * spin_color
    return pl.pallas_call(
        pick_kernel,
        out_shape=jax.ShapeDtypeStruct((rows, mode_count), vectors.dtype),
        in_specs=[pl.BlockSpec(memory_space=pl.ANY)] * 2,
        out_specs=pl.BlockSpec(memory_space=pltpu.VMEM),
        scratch_shapes=[
            pltpu.SMEM(source_sites.shape, source_sites.dtype),
            pltpu.VMEM((source_count, parts, spin_color, mode_count, LANES), vectors.dtype),
            pltpu.VMEM((rows, mode_count), jnp.float32),
            pltpu.SemaphoreType.DMA,
            pltpu.SemaphoreType.DMA((source_count, parts)),
        ],
        compiler_params=pltpu.CompilerParams(vmem_limit_bytes=24 * MIB),
        name="pick",
    )(source_sites, vectors)


def load(vectors, after, start, count):
    parts, spin_color, mode_count, site_count = vectors.shape

    def load_kernel(vectors_ref, after_ref, held_ref, sems):
        copies = [
            pltpu.make_async_copy(vectors_ref.at[part, pl.ds(start, count)], held_ref.at[part], sems.at[part])
            for part in range(parts)
        ]
        for copy in copies:
            copy.start()
        for copy in copies:
            copy.wait()

    shape = (parts, count, mode_count, site_count)
    size = 2 * parts * count * mode_count * site_count
    return pl.pallas_call(
        load_kernel,
        out_shape=jax.ShapeDtypeStruct(shape, vectors.dtype),
        in_specs=[pl.BlockSpec(memory_space=pl.ANY)] * 2,
        out_specs=pl.BlockSpec(memory_space=pltpu.VMEM),
        scratch_shapes=[pltpu.SemaphoreType.DMA((parts,))],
        compiler_params=pltpu.CompilerParams(vmem_limit_bytes=40 * MIB),
        cost_estimate=pl.CostEstimate(flops=0, bytes_accessed=2 * size, transcendentals=0),
        name="load",
    )(vectors, after)


def iota(shape, dim):
    return lax.broadcasted_iota(jnp.int32, shape, dim)


def shares(columns, ways, core, plane):
    share = columns // ways
    shape = (2 * columns, 2 * columns)
    row, entry = iota(shape, 0), iota(shape, 1)
    place, inner = row // (2 * share), row % (2 * share)
    its_core = jnp.where(place < 2, 1 - core, core)
    its_plane = jnp.where((place == 0) | (place == 3), plane, 1 - plane)
    column, part = (2 * its_plane + its_core) * share + inner // 2, inner % 2
    real, imag = (entry == column), (entry == column + columns)
    one = jnp.float32(1)
    zero = jnp.float32(0)
    on_real = jnp.where(part == 0, jnp.where(real, one, zero), jnp.where(imag, one, zero))
    on_imag = jnp.where(part == 0, jnp.where(imag, -one, zero), jnp.where(real, one, zero))
    return on_real.astype(jnp.bfloat16), on_imag.astype(jnp.bfloat16)


def dot(left, right):
    return jnp.dot(left, right, preferred_element_type=jnp.float32)


def project_kernel(rows_ref, values_ref, *refs):
    vectors_refs, (sent_ref, kept_ref, flat_ref) = refs[:-3], refs[-3:]
    columns = rows_ref.shape[0] // 2
    ways = 4
    share = 2 * columns // ways
    index = lax.axis_index("modes")
    divisor = values_ref[...]
    real = rows_ref[:columns, :].astype(jnp.float32) / divisor
    imag = -rows_ref[columns:, :].astype(jnp.float32) / divisor
    weights = jnp.concatenate([real, imag], axis=0).astype(jnp.bfloat16)
    on_real, on_imag = shares(columns, ways, index % 2, index // 2)
    left_real = dot(on_real, weights).astype(jnp.bfloat16)
    left_imag = dot(on_imag, weights).astype(jnp.bfloat16)
    component = 0
    for vectors_ref in vectors_refs:
        for inner in range(vectors_ref.shape[1]):
            product = dot(left_real, vectors_ref[0, inner]) + dot(left_imag, vectors_ref[1, inner])
            for place in range(ways):
                flat_ref[place, pl.ds(component * share, share), :] = product[place * share:(place + 1) * share]
            component += 1
    sent_ref[...] = flat_ref[:2].astype(sent_ref.dtype)
    kept_ref[...] = flat_ref[2:].astype(kept_ref.dtype)


def project(rows, eigenvalues, pieces):
    mode_count, site_count = pieces[0].shape[2:]
    spin_color = sum(piece.shape[1] for piece in pieces)
    share = rows.shape[0] // 4 * spin_color
    shape = (2, share, site_count)
    return pl.pallas_call(
        project_kernel,
        out_shape=[jax.ShapeDtypeStruct(shape, jnp.bfloat16), jax.ShapeDtypeStruct(shape, jnp.float32)],
        in_specs=[pl.BlockSpec(memory_space=pltpu.VMEM)] * (2 + len(pieces)),
        out_specs=[pl.BlockSpec(memory_space=pltpu.VMEM)] * 2,
        scratch_shapes=[pltpu.VMEM((4, share, site_count), jnp.float32)],
        compiler_params=pltpu.CompilerParams(vmem_limit_bytes=32 * MIB),
        name="project",
    )(rows, eigenvalues.reshape(1, mode_count), *pieces)


def swap(block, axis, size, bit):
    return lax.ppermute(block, axis, [(index, index ^ bit) for index in range(size)])


def on_device(eigvecs, eigenvalues, source_sites):
    site_ways, mode_ways = lax.axis_size("sites"), lax.axis_size("modes")
    vectors = jnp.transpose(eigvecs, (0, 2, 1, 3))
    parts, spin_color, mode_count, site_count = vectors.shape
    rows = pick(pltpu.with_memory_space_constraint(source_sites, pltpu.HBM), pltpu.with_memory_space_constraint(vectors, pltpu.HBM))
    groups = list(GROUPS)
    bit = 8
    while bit < site_ways:
        groups.append([bit])
        bit *= 2
    pieces = []
    step = spin_color // len(GROUPS)
    for number, group in enumerate(groups):
        if number < len(GROUPS):
            pass
        for block in [swap(rows, "sites", site_ways, bit) for bit in group]:
            rows = rows + block
    pieces = [pltpu.with_memory_space_constraint(vectors, pltpu.VMEM)]
    sent, kept = project(rows, eigenvalues, pieces)
    got = swap(sent, "modes", mode_ways, 1)
    across = (kept[0] + got[1].astype(jnp.float32)).astype(jnp.bfloat16)
    arrived = swap(across, "modes", mode_ways, 2)
    total = kept[1] + got[0].astype(jnp.float32) + arrived.astype(jnp.float32)
    share = total.shape[0] // spin_color // 2
    return jnp.transpose(total.reshape(spin_color, share, 2, site_count), (1, 2, 0, 3))


def solution(mesh):
    in_specs = (P(None, "modes", None, "sites"), P("modes"), P())
    out_specs = P("modes", None, None, "sites")
    return jax.shard_map(on_device, mesh=mesh, in_specs=in_specs, out_specs=out_specs, check_vma=False)
```

```python
import functools

import jax
import jax.numpy as jnp
from jax import lax
from jax.experimental import pallas as pl
from jax.experimental.pallas import tpu as pltpu
from jax.sharding import PartitionSpec as P

LANES = 128
MIB = 2**20
ROWS = 128
FIRST = 4
GROUPS = [[1], [2, 4, 6]]


def pick_kernel(given_ref, vectors_ref, rows_ref, sites_ref, columns_ref, total_ref, given_sem, sems):
    given = pltpu.make_async_copy(given_ref, sites_ref, given_sem)
    given.start()
    total_ref[...] = jnp.zeros_like(total_ref)
    given.wait()
    parts, spin_color, mode_count, site_count = vectors_ref.shape
    source_count = sites_ref.shape[0]
    first = lax.axis_index("sites") * site_count
    local = [sites_ref[number] - first for number in range(source_count)]
    held = [(index >= 0) & (index < site_count) for index in local]

    def copy(number, part):
        start = pl.multiple_of(local[number] // LANES * LANES, LANES)
        return pltpu.make_async_copy(
            vectors_ref.at[part, :, :, pl.ds(start, LANES)],
            columns_ref.at[number, part],
            sems.at[number, part],
        )

    for number in range(source_count):
        @pl.when(held[number])
        def _(number=number):
            for part in range(parts):
                copy(number, part).start()

    lane = lax.broadcasted_iota(jnp.int32, (8, LANES), 1)
    for number in range(source_count):
        @pl.when(held[number])
        def _(number=number):
            chosen = jnp.where(lane == local[number] % LANES, 1.0, 0.0).astype(jnp.bfloat16)
            for part in range(parts):
                copy(number, part).wait()
                row = lax.dot_general(
                    chosen,
                    columns_ref[number, part].reshape(spin_color * mode_count, LANES),
                    (((1,), (1,)), ((), ())),
                    preferred_element_type=jnp.float32,
                )
                base = (part * source_count + number) * spin_color
                for component in range(spin_color):
                    total_ref[base + component, :] = row[0, component * mode_count:(component + 1) * mode_count]
    rows_ref[...] = total_ref[...].astype(rows_ref.dtype)


def pick(source_sites, vectors):
    parts, spin_color, mode_count, site_count = vectors.shape
    source_count = source_sites.shape[0]
    rows = parts * source_count * spin_color
    return pl.pallas_call(
        pick_kernel,
        out_shape=jax.ShapeDtypeStruct((rows, mode_count), vectors.dtype),
        in_specs=[pl.BlockSpec(memory_space=pl.ANY)] * 2,
        out_specs=pl.BlockSpec(memory_space=pltpu.VMEM),
        scratch_shapes=[
            pltpu.SMEM(source_sites.shape, source_sites.dtype),
            pltpu.VMEM((source_count, parts, spin_color, mode_count, LANES), vectors.dtype),
            pltpu.VMEM((rows, mode_count), jnp.float32),
            pltpu.SemaphoreType.DMA,
            pltpu.SemaphoreType.DMA((source_count, parts)),
        ],
        compiler_params=pltpu.CompilerParams(vmem_limit_bytes=24 * MIB),
        name="pick",
    )(source_sites, vectors)


def load(vectors, after, start, count):
    parts, spin_color, mode_count, site_count = vectors.shape

    def load_kernel(vectors_ref, after_ref, held_ref, sems):
        copies = [
            pltpu.make_async_copy(vectors_ref.at[part, pl.ds(start, count)], held_ref.at[part], sems.at[part])
            for part in range(parts)
        ]
        for copy in copies:
            copy.start()
        for copy in copies:
            copy.wait()

    shape = (parts, count, mode_count, site_count)
    size = 2 * parts * count * mode_count * site_count
    return pl.pallas_call(
        load_kernel,
        out_shape=jax.ShapeDtypeStruct(shape, vectors.dtype),
        in_specs=[pl.BlockSpec(memory_space=pl.ANY)] * 2,
        out_specs=pl.BlockSpec(memory_space=pltpu.VMEM),
        scratch_shapes=[pltpu.SemaphoreType.DMA((parts,))],
        compiler_params=pltpu.CompilerParams(vmem_limit_bytes=40 * MIB),
        cost_estimate=pl.CostEstimate(flops=0, bytes_accessed=2 * size, transcendentals=0),
        name="load",
    )(vectors, after)


def iota(shape, dim):
    return lax.broadcasted_iota(jnp.int32, shape, dim)


def shares(columns, ways, core, plane):
    share = columns // ways
    shape = (2 * columns, 2 * columns)
    row, entry = iota(shape, 0), iota(shape, 1)
    place, inner = row // (2 * share), row % (2 * share)
    its_core = jnp.where(place < 2, 1 - core, core)
    its_plane = jnp.where((place == 0) | (place == 3), plane, 1 - plane)
    column, part = (2 * its_plane + its_core) * share + inner // 2, inner % 2
    real, imag = (entry == column), (entry == column + columns)
    one = jnp.float32(1)
    zero = jnp.float32(0)
    on_real = jnp.where(part == 0, jnp.where(real, one, zero), jnp.where(imag, one, zero))
    on_imag = jnp.where(part == 0, jnp.where(imag, -one, zero), jnp.where(real, one, zero))
    return on_real.astype(jnp.bfloat16), on_imag.astype(jnp.bfloat16)


def dot(left, right):
    return jnp.dot(left, right, preferred_element_type=jnp.float32)


def multiply(left, vectors_ref, start, sent_ref, kept_ref, flat_ref, share):
    count = flat_ref.shape[1] // share
    for inner in range(count):
        component = start + inner
        product = dot(left[0], vectors_ref[0, component]) + dot(left[1], vectors_ref[1, component])
        for place in range(flat_ref.shape[0]):
            flat_ref[place, pl.ds(inner * share, share), :] = product[place * share:(place + 1) * share]
    sent_ref[...] = flat_ref[:2].astype(sent_ref.dtype)
    kept_ref[...] = flat_ref[2:].astype(kept_ref.dtype)


def first_kernel(rows_ref, values_ref, vectors_ref, sent_ref, kept_ref, left_ref, flat_ref):
    columns = rows_ref.shape[0] // 2
    ways = flat_ref.shape[0]
    index = lax.axis_index("modes")
    divisor = values_ref[...]
    real = rows_ref[:columns, :].astype(jnp.float32) / divisor
    imag = -rows_ref[columns:, :].astype(jnp.float32) / divisor
    weights = jnp.concatenate([real, imag], axis=0).astype(jnp.bfloat16)
    on_real, on_imag = shares(columns, ways, index % 2, index // 2)
    spare = jnp.zeros((ROWS - 2 * columns, weights.shape[1]), jnp.bfloat16)
    left = [jnp.concatenate([dot(on, weights).astype(jnp.bfloat16), spare], axis=0) for on in (on_real, on_imag)]
    left_ref[0] = left[0]
    left_ref[1] = left[1]
    multiply(left, vectors_ref, 0, sent_ref, kept_ref, flat_ref, 2 * columns // ways)


def next_kernel(start, left_ref, vectors_ref, sent_ref, kept_ref, flat_ref):
    share = flat_ref.shape[1] // (vectors_ref.shape[1] - start)
    multiply([left_ref[0], left_ref[1]], vectors_ref, start, sent_ref, kept_ref, flat_ref, share)


def project(rows, eigenvalues, vectors, ways):
    parts, spin_color, mode_count, site_count = vectors.shape
    share = rows.shape[0] // ways
    vmem = pl.BlockSpec(memory_space=pltpu.VMEM)

    def call(kernel, operands, count, extra, name):
        shape = (2, count * share, site_count)
        size = 2 * parts * count * mode_count * site_count
        return pl.pallas_call(
            kernel,
            out_shape=[jax.ShapeDtypeStruct(shape, jnp.bfloat16), jax.ShapeDtypeStruct(shape, jnp.float32)] + extra,
            in_specs=[vmem] * len(operands),
            out_specs=[vmem] * (2 + len(extra)),
            scratch_shapes=[pltpu.VMEM((ways, count * share, site_count), jnp.float32)],
            compiler_params=pltpu.CompilerParams(vmem_limit_bytes=24 * MIB),
            cost_estimate=pl.CostEstimate(flops=size * ROWS, bytes_accessed=size, transcendentals=0),
            name=name,
        )(*operands)

    left = jax.ShapeDtypeStruct((2, ROWS, mode_count), jnp.bfloat16)
    *first, left = call(first_kernel, (rows, eigenvalues.reshape(1, mode_count), vectors), FIRST, [left], "first")
    rest = call(functools.partial(next_kernel, FIRST), (left, vectors), spin_color - FIRST, [], "rest")
    return [first, rest]


def swap(block, axis, size, bit):
    return lax.ppermute(block, axis, [(index, index ^ bit) for index in range(size)])


def on_device(eigvecs, eigenvalues, source_sites):
    site_ways, mode_ways = lax.axis_size("sites"), lax.axis_size("modes")
    vectors = jnp.transpose(eigvecs, (0, 2, 1, 3))
    parts, spin_color, mode_count, site_count = vectors.shape
    rows = pick(pltpu.with_memory_space_constraint(source_sites, pltpu.HBM), pltpu.with_memory_space_constraint(vectors, pltpu.HBM))
    groups = list(GROUPS)
    bit = 8
    while bit < site_ways:
        groups.append([bit])
        bit *= 2
    pieces = []
    step = spin_color // len(GROUPS)
    for number, group in enumerate(groups):
        if number < len(GROUPS):
            pass
        for block in [swap(rows, "sites", site_ways, bit) for bit in group]:
            rows = rows + block
    halves = []
    for sent, kept in project(rows, eigenvalues, pltpu.with_memory_space_constraint(vectors, pltpu.VMEM), mode_ways):
        got = swap(sent, "modes", mode_ways, 1)
        across = (kept[0] + got[1].astype(jnp.float32)).astype(jnp.bfloat16)
        arrived = swap(across, "modes", mode_ways, 2)
        halves.append(kept[1] + got[0].astype(jnp.float32) + arrived.astype(jnp.float32))
    total = jnp.concatenate(halves, axis=0)
    share = total.shape[0] // spin_color // 2
    return jnp.transpose(total.reshape(spin_color, share, 2, site_count), (1, 2, 0, 3))


def solution(mesh):
    in_specs = (P(None, "modes", None, "sites"), P("modes"), P())
    out_specs = P("modes", None, None, "sites")
    return jax.shard_map(on_device, mesh=mesh, in_specs=in_specs, out_specs=out_specs, check_vma=False)
```

```python
import functools

import jax
import jax.numpy as jnp
from jax import lax
from jax.experimental import pallas as pl
from jax.experimental.pallas import tpu as pltpu
from jax.sharding import PartitionSpec as P

LANES = 128
MIB = 2**20
ROWS = 128
STEPS = (6, 6)
GROUPS = [[1], [2, 4, 6]]


def pick_kernel(given_ref, vectors_ref, rows_ref, sites_ref, columns_ref, total_ref, given_sem, sems):
    given = pltpu.make_async_copy(given_ref, sites_ref, given_sem)
    given.start()
    total_ref[...] = jnp.zeros_like(total_ref)
    given.wait()
    parts, spin_color, mode_count, site_count = vectors_ref.shape
    source_count = sites_ref.shape[0]
    first = lax.axis_index("sites") * site_count
    local = [sites_ref[number] - first for number in range(source_count)]
    held = [(index >= 0) & (index < site_count) for index in local]

    def copy(number, part):
        start = pl.multiple_of(local[number] // LANES * LANES, LANES)
        return pltpu.make_async_copy(
            vectors_ref.at[part, :, :, pl.ds(start, LANES)],
            columns_ref.at[number, part],
            sems.at[number, part],
        )

    for number in range(source_count):
        @pl.when(held[number])
        def _(number=number):
            for part in range(parts):
                copy(number, part).start()

    lane = lax.broadcasted_iota(jnp.int32, (8, LANES), 1)
    for number in range(source_count):
        @pl.when(held[number])
        def _(number=number):
            chosen = jnp.where(lane == local[number] % LANES, 1.0, 0.0).astype(jnp.bfloat16)
            for part in range(parts):
                copy(number, part).wait()
                row = lax.dot_general(
                    chosen,
                    columns_ref[number, part].reshape(spin_color * mode_count, LANES),
                    (((1,), (1,)), ((), ())),
                    preferred_element_type=jnp.float32,
                )
                base = (part * source_count + number) * spin_color
                for component in range(spin_color):
                    total_ref[base + component, :] = row[0, component * mode_count:(component + 1) * mode_count]
    rows_ref[...] = total_ref[...].astype(rows_ref.dtype)


def pick(source_sites, vectors):
    parts, spin_color, mode_count, site_count = vectors.shape
    source_count = source_sites.shape[0]
    rows = parts * source_count * spin_color
    return pl.pallas_call(
        pick_kernel,
        out_shape=jax.ShapeDtypeStruct((rows, mode_count), vectors.dtype),
        in_specs=[pl.BlockSpec(memory_space=pl.ANY)] * 2,
        out_specs=pl.BlockSpec(memory_space=pltpu.VMEM),
        scratch_shapes=[
            pltpu.SMEM(source_sites.shape, source_sites.dtype),
            pltpu.VMEM((source_count, parts, spin_color, mode_count, LANES), vectors.dtype),
            pltpu.VMEM((rows, mode_count), jnp.float32),
            pltpu.SemaphoreType.DMA,
            pltpu.SemaphoreType.DMA((source_count, parts)),
        ],
        compiler_params=pltpu.CompilerParams(vmem_limit_bytes=24 * MIB),
        name="pick",
    )(source_sites, vectors)


def load(vectors, after, start, count):
    parts, spin_color, mode_count, site_count = vectors.shape

    def load_kernel(vectors_ref, after_ref, held_ref, sems):
        copies = [
            pltpu.make_async_copy(vectors_ref.at[part, pl.ds(start, count)], held_ref.at[part], sems.at[part])
            for part in range(parts)
        ]
        for copy in copies:
            copy.start()
        for copy in copies:
            copy.wait()

    shape = (parts, count, mode_count, site_count)
    size = 2 * parts * count * mode_count * site_count
    return pl.pallas_call(
        load_kernel,
        out_shape=jax.ShapeDtypeStruct(shape, vectors.dtype),
        in_specs=[pl.BlockSpec(memory_space=pl.ANY)] * 2,
        out_specs=pl.BlockSpec(memory_space=pltpu.VMEM),
        scratch_shapes=[pltpu.SemaphoreType.DMA((parts,))],
        compiler_params=pltpu.CompilerParams(vmem_limit_bytes=40 * MIB),
        cost_estimate=pl.CostEstimate(flops=0, bytes_accessed=2 * size, transcendentals=0),
        name="load",
    )(vectors, after)


def iota(shape, dim):
    return lax.broadcasted_iota(jnp.int32, shape, dim)


def shares(columns, ways, core, plane):
    share = columns // ways
    shape = (2 * columns, 2 * columns)
    row, entry = iota(shape, 0), iota(shape, 1)
    place, inner = row // (2 * share), row % (2 * share)
    its_core = jnp.where(place % 2 == 0, 1 - core, core)
    its_plane = jnp.where((place == 0) | (place == 3), plane, 1 - plane)
    column, part = (2 * its_plane + its_core) * share + inner // 2, inner % 2
    real, imag = (entry == column), (entry == column + columns)
    one = jnp.float32(1)
    zero = jnp.float32(0)
    on_real = jnp.where(part == 0, jnp.where(real, one, zero), jnp.where(imag, one, zero))
    on_imag = jnp.where(part == 0, jnp.where(imag, -one, zero), jnp.where(real, one, zero))
    return on_real.astype(jnp.bfloat16), on_imag.astype(jnp.bfloat16)


def dot(left, right):
    return jnp.dot(left, right, preferred_element_type=jnp.float32)


def multiply(left, vectors_ref, start, sent_ref, kept_ref, flat_ref, share):
    count = flat_ref.shape[1] // share
    for inner in range(count):
        component = start + inner
        product = dot(left[0], vectors_ref[0, component]) + dot(left[1], vectors_ref[1, component])
        for place in range(flat_ref.shape[0]):
            flat_ref[place, pl.ds(inner * share, share), :] = product[place * share:(place + 1) * share]
    sent_ref[...] = flat_ref[:2].astype(sent_ref.dtype)
    kept_ref[...] = flat_ref[2:].astype(kept_ref.dtype)


def first_kernel(rows_ref, values_ref, vectors_ref, sent_ref, kept_ref, left_ref, flat_ref):
    columns = rows_ref.shape[0] // 2
    ways = flat_ref.shape[0]
    index = lax.axis_index("modes")
    divisor = values_ref[...]
    real = rows_ref[:columns, :].astype(jnp.float32) / divisor
    imag = -rows_ref[columns:, :].astype(jnp.float32) / divisor
    weights = jnp.concatenate([real, imag], axis=0).astype(jnp.bfloat16)
    on_real, on_imag = shares(columns, ways, index % 2, index // 2)
    spare = jnp.zeros((ROWS - 2 * columns, weights.shape[1]), jnp.bfloat16)
    left = [jnp.concatenate([dot(on, weights).astype(jnp.bfloat16), spare], axis=0) for on in (on_real, on_imag)]
    left_ref[0] = left[0]
    left_ref[1] = left[1]
    multiply(left, vectors_ref, 0, sent_ref, kept_ref, flat_ref, 2 * columns // ways)


def next_kernel(start, left_ref, vectors_ref, sent_ref, kept_ref, flat_ref):
    share = 12
    multiply([left_ref[0], left_ref[1]], vectors_ref, start, sent_ref, kept_ref, flat_ref, share)


def project(rows, eigenvalues, vectors, ways):
    parts, spin_color, mode_count, site_count = vectors.shape
    share = rows.shape[0] // ways
    vmem = pl.BlockSpec(memory_space=pltpu.VMEM)

    def call(kernel, operands, count, extra, name):
        shape = (2, count * share, site_count)
        size = 2 * parts * count * mode_count * site_count
        return pl.pallas_call(
            kernel,
            out_shape=[jax.ShapeDtypeStruct(shape, jnp.bfloat16), jax.ShapeDtypeStruct(shape, jnp.float32)] + extra,
            in_specs=[vmem] * len(operands),
            out_specs=[vmem] * (2 + len(extra)),
            scratch_shapes=[pltpu.VMEM((ways, count * share, site_count), jnp.float32)],
            compiler_params=pltpu.CompilerParams(vmem_limit_bytes=24 * MIB),
            cost_estimate=pl.CostEstimate(flops=size * ROWS, bytes_accessed=size, transcendentals=0),
            name=name,
        )(*operands)

    left = jax.ShapeDtypeStruct((2, ROWS, mode_count), jnp.bfloat16)
    *first, left = call(first_kernel, (rows, eigenvalues.reshape(1, mode_count), vectors), STEPS[0], [left], "first")
    results = [first]
    start = STEPS[0]
    for count in STEPS[1:]:
        results.append(call(functools.partial(next_kernel, start), (left, vectors), count, [], "rest"))
        start += count
    return results


def swap(block, axis, size, bit):
    return lax.ppermute(block, axis, [(index, index ^ bit) for index in range(size)])


def on_device(eigvecs, eigenvalues, source_sites):
    site_ways, mode_ways = lax.axis_size("sites"), lax.axis_size("modes")
    vectors = jnp.transpose(eigvecs, (0, 2, 1, 3))
    parts, spin_color, mode_count, site_count = vectors.shape
    rows = pick(pltpu.with_memory_space_constraint(source_sites, pltpu.HBM), pltpu.with_memory_space_constraint(vectors, pltpu.HBM))
    groups = list(GROUPS)
    bit = 8
    while bit < site_ways:
        groups.append([bit])
        bit *= 2
    pieces = []
    step = spin_color // len(GROUPS)
    for number, group in enumerate(groups):
        if number < len(GROUPS):
            pass
        for block in [swap(rows, "sites", site_ways, bit) for bit in group]:
            rows = rows + block
    halves = []
    for sent, kept in project(rows, eigenvalues, pltpu.with_memory_space_constraint(vectors, pltpu.VMEM), mode_ways):
        got = swap(sent, "modes", mode_ways, 1)
        across = (kept[0] + got[1].astype(jnp.float32)).astype(jnp.bfloat16)
        arrived = swap(across, "modes", mode_ways, 3)
        halves.append(kept[1] + got[0].astype(jnp.float32) + arrived.astype(jnp.float32))
    total = jnp.concatenate(halves, axis=0)
    share = total.shape[0] // spin_color // 2
    return jnp.transpose(total.reshape(spin_color, share, 2, site_count), (1, 2, 0, 3))


def solution(mesh):
    in_specs = (P(None, "modes", None, "sites"), P("modes"), P())
    out_specs = P("modes", None, None, "sites")
    return jax.shard_map(on_device, mesh=mesh, in_specs=in_specs, out_specs=out_specs, check_vma=False)
```

```python
import functools

import jax
import jax.numpy as jnp
from jax import lax
from jax.experimental import pallas as pl
from jax.experimental.pallas import tpu as pltpu
from jax.sharding import PartitionSpec as P

LANES = 128
MIB = 2**20
ROWS = 128
STEPS = (6, 6)


def pick_kernel(given_ref, vectors_ref, rows_ref, sites_ref, columns_ref, total_ref, given_sem, sems):
    given = pltpu.make_async_copy(given_ref, sites_ref, given_sem)
    given.start()
    total_ref[...] = jnp.zeros_like(total_ref)
    given.wait()
    parts, spin_color, mode_count, site_count = vectors_ref.shape
    source_count = sites_ref.shape[0]
    first = lax.axis_index("sites") * site_count
    local = [sites_ref[number] - first for number in range(source_count)]
    held = [(index >= 0) & (index < site_count) for index in local]

    def copy(number, part):
        start = pl.multiple_of(local[number] // LANES * LANES, LANES)
        return pltpu.make_async_copy(
            vectors_ref.at[part, :, :, pl.ds(start, LANES)],
            columns_ref.at[number, part],
            sems.at[number, part],
        )

    for number in range(source_count):
        @pl.when(held[number])
        def _(number=number):
            for part in range(parts):
                copy(number, part).start()

    lane = lax.broadcasted_iota(jnp.int32, (8, LANES), 1)
    for number in range(source_count):
        @pl.when(held[number])
        def _(number=number):
            chosen = jnp.where(lane == local[number] % LANES, 1.0, 0.0).astype(jnp.bfloat16)
            for part in range(parts):
                copy(number, part).wait()
                row = lax.dot_general(
                    chosen,
                    columns_ref[number, part].reshape(spin_color * mode_count, LANES),
                    (((1,), (1,)), ((), ())),
                    preferred_element_type=jnp.float32,
                )
                base = (part * source_count + number) * spin_color
                for component in range(spin_color):
                    total_ref[base + component, :] = row[0, component * mode_count:(component + 1) * mode_count]
    rows_ref[...] = total_ref[...].astype(rows_ref.dtype)


def pick(source_sites, vectors):
    parts, spin_color, mode_count, site_count = vectors.shape
    source_count = source_sites.shape[0]
    rows = parts * source_count * spin_color
    return pl.pallas_call(
        pick_kernel,
        out_shape=jax.ShapeDtypeStruct((rows, mode_count), vectors.dtype),
        in_specs=[pl.BlockSpec(memory_space=pl.ANY)] * 2,
        out_specs=pl.BlockSpec(memory_space=pltpu.VMEM),
        scratch_shapes=[
            pltpu.SMEM(source_sites.shape, source_sites.dtype),
            pltpu.VMEM((source_count, parts, spin_color, mode_count, LANES), vectors.dtype),
            pltpu.VMEM((rows, mode_count), jnp.float32),
            pltpu.SemaphoreType.DMA,
            pltpu.SemaphoreType.DMA((source_count, parts)),
        ],
        compiler_params=pltpu.CompilerParams(vmem_limit_bytes=24 * MIB),
        name="pick",
    )(source_sites, vectors)


def iota(shape, dim):
    return lax.broadcasted_iota(jnp.int32, shape, dim)


def shares(columns, ways, core, plane):
    share = columns // ways
    shape = (2 * columns, 2 * columns)
    row, entry = iota(shape, 0), iota(shape, 1)
    place, inner = row // (2 * share), row % (2 * share)
    its_core = jnp.where(place % 2 == 0, 1 - core, core)
    its_plane = jnp.where((place == 0) | (place == 3), plane, 1 - plane)
    column, part = (2 * its_plane + its_core) * share + inner // 2, inner % 2
    real, imag = (entry == column), (entry == column + columns)
    one = jnp.float32(1)
    zero = jnp.float32(0)
    on_real = jnp.where(part == 0, jnp.where(real, one, zero), jnp.where(imag, one, zero))
    on_imag = jnp.where(part == 0, jnp.where(imag, -one, zero), jnp.where(real, one, zero))
    return on_real.astype(jnp.bfloat16), on_imag.astype(jnp.bfloat16)


def dot(left, right):
    return jnp.dot(left, right, preferred_element_type=jnp.float32)


def multiply(left, vectors_ref, start, sent_ref, kept_ref, flat_ref, share):
    count = flat_ref.shape[1] // share
    for inner in range(count):
        component = start + inner
        product = dot(left[0], vectors_ref[0, component]) + dot(left[1], vectors_ref[1, component])
        for place in range(flat_ref.shape[0]):
            flat_ref[place, pl.ds(inner * share, share), :] = product[place * share:(place + 1) * share]
    sent_ref[...] = flat_ref[:2].astype(sent_ref.dtype)
    kept_ref[...] = flat_ref[2:].astype(kept_ref.dtype)


def first_kernel(rows_ref, values_ref, vectors_ref, sent_ref, kept_ref, left_ref, flat_ref):
    columns = rows_ref.shape[0] // 2
    ways = flat_ref.shape[0]
    index = lax.axis_index("modes")
    divisor = values_ref[...]
    real = rows_ref[:columns, :].astype(jnp.float32) / divisor
    imag = -rows_ref[columns:, :].astype(jnp.float32) / divisor
    weights = jnp.concatenate([real, imag], axis=0).astype(jnp.bfloat16)
    on_real, on_imag = shares(columns, ways, index % 2, index // 2)
    spare = jnp.zeros((ROWS - 2 * columns, weights.shape[1]), jnp.bfloat16)
    left = [jnp.concatenate([dot(on, weights).astype(jnp.bfloat16), spare], axis=0) for on in (on_real, on_imag)]
    left_ref[0] = left[0]
    left_ref[1] = left[1]
    multiply(left, vectors_ref, 0, sent_ref, kept_ref, flat_ref, 2 * columns // ways)


def next_kernel(start, share, left_ref, vectors_ref, sent_ref, kept_ref, flat_ref):
    multiply([left_ref[0], left_ref[1]], vectors_ref, start, sent_ref, kept_ref, flat_ref, share)


def project(rows, eigenvalues, vectors, ways):
    parts, spin_color, mode_count, site_count = vectors.shape
    share = rows.shape[0] // ways
    vmem = pl.BlockSpec(memory_space=pltpu.VMEM)

    def call(kernel, operands, count, extra, name):
        shape = (2, count * share, site_count)
        size = 2 * parts * count * mode_count * site_count
        return pl.pallas_call(
            kernel,
            out_shape=[jax.ShapeDtypeStruct(shape, jnp.bfloat16), jax.ShapeDtypeStruct(shape, jnp.float32)] + extra,
            in_specs=[vmem] * len(operands),
            out_specs=[vmem] * (2 + len(extra)),
            scratch_shapes=[pltpu.VMEM((ways, count * share, site_count), jnp.float32)],
            compiler_params=pltpu.CompilerParams(vmem_limit_bytes=24 * MIB),
            cost_estimate=pl.CostEstimate(flops=size * ROWS, bytes_accessed=size, transcendentals=0),
            name=name,
        )(*operands)

    left = jax.ShapeDtypeStruct((2, ROWS, mode_count), jnp.bfloat16)
    *first, left = call(first_kernel, (rows, eigenvalues.reshape(1, mode_count), vectors), STEPS[0], [left], "first")
    results = [first]
    start = STEPS[0]
    for count in STEPS[1:]:
        results.append(call(functools.partial(next_kernel, start, share), (left, vectors), count, [], "rest"))
        start += count
    return results


def swap(block, axis, size, bit):
    return lax.ppermute(block, axis, [(index, index ^ bit) for index in range(size)])


def on_device(eigvecs, eigenvalues, source_sites):
    site_ways, mode_ways = lax.axis_size("sites"), lax.axis_size("modes")
    vectors = jnp.transpose(eigvecs, (0, 2, 1, 3))
    parts, spin_color, mode_count, site_count = vectors.shape
    rows = pick(pltpu.with_memory_space_constraint(source_sites, pltpu.HBM), pltpu.with_memory_space_constraint(vectors, pltpu.HBM))
    near = swap(rows, "sites", site_ways, 6)
    far = [swap(rows, "sites", site_ways, bit) for bit in (5, 3)]
    pair = rows + near
    late = [swap(pair, "sites", site_ways, bit) for bit in (1, 2)]
    rows = pair
    for block in far + late:
        rows = rows + block
    bit = 8
    while bit < site_ways:
        rows = rows + swap(rows, "sites", site_ways, bit)
        bit *= 2
    halves = []
    for sent, kept in project(rows, eigenvalues, pltpu.with_memory_space_constraint(vectors, pltpu.VMEM), mode_ways):
        got = swap(sent, "modes", mode_ways, 1)
        across = (kept[0] + got[1].astype(jnp.float32)).astype(jnp.bfloat16)
        arrived = swap(across, "modes", mode_ways, 3)
        halves.append(kept[1] + got[0].astype(jnp.float32) + arrived.astype(jnp.float32))
    total = jnp.concatenate(halves, axis=0)
    share = total.shape[0] // spin_color // 2
    return jnp.transpose(total.reshape(spin_color, share, 2, site_count), (1, 2, 0, 3))


def solution(mesh):
    in_specs = (P(None, "modes", None, "sites"), P("modes"), P())
    out_specs = P("modes", None, None, "sites")
    return jax.shard_map(on_device, mesh=mesh, in_specs=in_specs, out_specs=out_specs, check_vma=False)
```

```python
import functools

import jax
import jax.numpy as jnp
from jax import lax
from jax.experimental import pallas as pl
from jax.experimental.pallas import tpu as pltpu
from jax.sharding import PartitionSpec as P

LANES = 128
MIB = 2**20
ROWS = 128
STEPS = (6, 6)


def pick_kernel(given_ref, values_ref, vectors_ref, rows_ref, sites_ref, divisor_ref, columns_ref, total_ref, given_sem, value_sem, sems):
    given = pltpu.make_async_copy(given_ref, sites_ref, given_sem)
    given.start()
    values = pltpu.make_async_copy(values_ref, divisor_ref, value_sem)
    values.start()
    total_ref[...] = jnp.zeros_like(total_ref)
    given.wait()
    parts, spin_color, mode_count, site_count = vectors_ref.shape
    source_count = sites_ref.shape[0]
    first = lax.axis_index("sites") * site_count
    local = [sites_ref[number] - first for number in range(source_count)]
    held = [(index >= 0) & (index < site_count) for index in local]

    def copy(number, part):
        start = pl.multiple_of(local[number] // LANES * LANES, LANES)
        return pltpu.make_async_copy(
            vectors_ref.at[part, :, :, pl.ds(start, LANES)],
            columns_ref.at[number, part],
            sems.at[number, part],
        )

    for number in range(source_count):
        @pl.when(held[number])
        def _(number=number):
            for part in range(parts):
                copy(number, part).start()

    lane = lax.broadcasted_iota(jnp.int32, (8, LANES), 1)
    for number in range(source_count):
        @pl.when(held[number])
        def _(number=number):
            chosen = jnp.where(lane == local[number] % LANES, 1.0, 0.0).astype(jnp.bfloat16)
            for part in range(parts):
                copy(number, part).wait()
                row = lax.dot_general(
                    chosen,
                    columns_ref[number, part].reshape(spin_color * mode_count, LANES),
                    (((1,), (1,)), ((), ())),
                    preferred_element_type=jnp.float32,
                )
                base = (part * source_count + number) * spin_color
                for component in range(spin_color):
                    total_ref[base + component, :] = row[0, component * mode_count:(component + 1) * mode_count]
    values.wait()
    divisor = divisor_ref[...]
    columns = source_count * spin_color
    real, imag = total_ref[:columns, :] / divisor, -total_ref[columns:, :] / divisor
    rows_ref[...] = jnp.concatenate([real, imag], axis=0).astype(rows_ref.dtype)


def pick(source_sites, eigenvalues, vectors):
    parts, spin_color, mode_count, site_count = vectors.shape
    source_count = source_sites.shape[0]
    rows = parts * source_count * spin_color
    return pl.pallas_call(
        pick_kernel,
        out_shape=jax.ShapeDtypeStruct((rows, mode_count), vectors.dtype),
        in_specs=[pl.BlockSpec(memory_space=pl.ANY)] * 3,
        out_specs=pl.BlockSpec(memory_space=pltpu.VMEM),
        scratch_shapes=[
            pltpu.SMEM(source_sites.shape, source_sites.dtype),
            pltpu.VMEM(eigenvalues.shape, eigenvalues.dtype),
            pltpu.VMEM((source_count, parts, spin_color, mode_count, LANES), vectors.dtype),
            pltpu.VMEM((rows, mode_count), jnp.float32),
            pltpu.SemaphoreType.DMA,
            pltpu.SemaphoreType.DMA,
            pltpu.SemaphoreType.DMA((source_count, parts)),
        ],
        compiler_params=pltpu.CompilerParams(vmem_limit_bytes=24 * MIB),
        name="pick",
    )(source_sites, eigenvalues, vectors)


def iota(shape, dim):
    return lax.broadcasted_iota(jnp.int32, shape, dim)


def shares(columns, ways, core, plane):
    share = columns // ways
    shape = (2 * columns, 2 * columns)
    row, entry = iota(shape, 0), iota(shape, 1)
    place, inner = row // (2 * share), row % (2 * share)
    its_core = jnp.where(place % 2 == 0, 1 - core, core)
    its_plane = jnp.where((place == 0) | (place == 3), plane, 1 - plane)
    column, part = (2 * its_plane + its_core) * share + inner // 2, inner % 2
    real, imag = (entry == column), (entry == column + columns)
    one = jnp.float32(1)
    zero = jnp.float32(0)
    on_real = jnp.where(part == 0, jnp.where(real, one, zero), jnp.where(imag, one, zero))
    on_imag = jnp.where(part == 0, jnp.where(imag, -one, zero), jnp.where(real, one, zero))
    return on_real.astype(jnp.bfloat16), on_imag.astype(jnp.bfloat16)


def dot(left, right):
    return jnp.dot(left, right, preferred_element_type=jnp.float32)


def multiply(left, vectors_ref, start, sent_ref, kept_ref, flat_ref, share):
    count = flat_ref.shape[1] // share
    for inner in range(count):
        component = start + inner
        product = dot(left[0], vectors_ref[0, component]) + dot(left[1], vectors_ref[1, component])
        for place in range(flat_ref.shape[0]):
            flat_ref[place, pl.ds(inner * share, share), :] = product[place * share:(place + 1) * share]
    sent_ref[...] = flat_ref[:2].astype(sent_ref.dtype)
    kept_ref[...] = flat_ref[2:].astype(kept_ref.dtype)


def first_kernel(rows_ref, vectors_ref, sent_ref, kept_ref, left_ref, flat_ref):
    columns = rows_ref.shape[0] // 2
    ways = flat_ref.shape[0]
    index = lax.axis_index("modes")
    weights = rows_ref[...]
    on_real, on_imag = shares(columns, ways, index % 2, index // 2)
    spare = jnp.zeros((ROWS - 2 * columns, weights.shape[1]), jnp.bfloat16)
    left = [jnp.concatenate([dot(on, weights).astype(jnp.bfloat16), spare], axis=0) for on in (on_real, on_imag)]
    left_ref[0] = left[0]
    left_ref[1] = left[1]
    multiply(left, vectors_ref, 0, sent_ref, kept_ref, flat_ref, 2 * columns // ways)


def next_kernel(start, share, left_ref, vectors_ref, sent_ref, kept_ref, flat_ref):
    multiply([left_ref[0], left_ref[1]], vectors_ref, start, sent_ref, kept_ref, flat_ref, share)


def project(rows, vectors, ways):
    parts, spin_color, mode_count, site_count = vectors.shape
    share = rows.shape[0] // ways
    vmem = pl.BlockSpec(memory_space=pltpu.VMEM)

    def call(kernel, operands, count, extra, name):
        shape = (2, count * share, site_count)
        size = 2 * parts * count * mode_count * site_count
        return pl.pallas_call(
            kernel,
            out_shape=[jax.ShapeDtypeStruct(shape, jnp.bfloat16), jax.ShapeDtypeStruct(shape, jnp.float32)] + extra,
            in_specs=[vmem] * len(operands),
            out_specs=[vmem] * (2 + len(extra)),
            scratch_shapes=[pltpu.VMEM((ways, count * share, site_count), jnp.float32)],
            compiler_params=pltpu.CompilerParams(vmem_limit_bytes=24 * MIB),
            cost_estimate=pl.CostEstimate(flops=size * ROWS, bytes_accessed=size, transcendentals=0),
            name=name,
        )(*operands)

    left = jax.ShapeDtypeStruct((2, ROWS, mode_count), jnp.bfloat16)
    *first, left = call(first_kernel, (rows, vectors), STEPS[0], [left], "first")
    results = [first]
    start = STEPS[0]
    for count in STEPS[1:]:
        results.append(call(functools.partial(next_kernel, start, share), (left, vectors), count, [], "rest"))
        start += count
    return results


def swap(block, axis, size, bit):
    return lax.ppermute(block, axis, [(index, index ^ bit) for index in range(size)])


def on_device(eigvecs, eigenvalues, source_sites):
    site_ways, mode_ways = lax.axis_size("sites"), lax.axis_size("modes")
    vectors = jnp.transpose(eigvecs, (0, 2, 1, 3))
    parts, spin_color, mode_count, site_count = vectors.shape
    operands = (source_sites, eigenvalues.reshape(1, mode_count), vectors)
    rows = pick(*[pltpu.with_memory_space_constraint(operand, pltpu.HBM) for operand in operands])
    near = swap(rows, "sites", site_ways, 6)
    far = [swap(rows, "sites", site_ways, bit) for bit in (5, 3)]
    pair = rows + near
    late = [swap(pair, "sites", site_ways, bit) for bit in (1, 2)]
    rows = pair
    for block in far + late:
        rows = rows + block
    bit = 8
    while bit < site_ways:
        rows = rows + swap(rows, "sites", site_ways, bit)
        bit *= 2
    halves = []
    for sent, kept in project(rows, pltpu.with_memory_space_constraint(vectors, pltpu.VMEM), mode_ways):
        got = swap(sent, "modes", mode_ways, 1)
        across = (kept[0] + got[1].astype(jnp.float32)).astype(jnp.bfloat16)
        arrived = swap(across, "modes", mode_ways, 3)
        halves.append(kept[1] + got[0].astype(jnp.float32) + arrived.astype(jnp.float32))
    total = jnp.concatenate(halves, axis=0)
    share = total.shape[0] // spin_color // 2
    return jnp.transpose(total.reshape(spin_color, share, 2, site_count), (1, 2, 0, 3))


def solution(mesh):
    in_specs = (P(None, "modes", None, "sites"), P("modes"), P())
    out_specs = P("modes", None, None, "sites")
    return jax.shard_map(on_device, mesh=mesh, in_specs=in_specs, out_specs=out_specs, check_vma=False)
```

```python
import functools

import jax
import jax.numpy as jnp
from jax import lax
from jax.experimental import pallas as pl
from jax.experimental.pallas import tpu as pltpu
from jax.sharding import PartitionSpec as P

LANES = 128
MIB = 2**20
ROWS = 128
STEPS = (6, 6)


def pick_kernel(given_ref, values_ref, vectors_ref, rows_ref, sites_ref, divisor_ref, columns_ref, total_ref, given_sem, value_sem, sems):
    given = pltpu.make_async_copy(given_ref, sites_ref, given_sem)
    given.start()
    values = pltpu.make_async_copy(values_ref, divisor_ref, value_sem)
    values.start()
    total_ref[...] = jnp.zeros_like(total_ref)
    given.wait()
    parts, spin_color, mode_count, site_count = vectors_ref.shape
    source_count = sites_ref.shape[0]
    first = lax.axis_index("sites") * site_count
    local = [sites_ref[number] - first for number in range(source_count)]
    held = [(index >= 0) & (index < site_count) for index in local]

    def copy(number, part):
        start = pl.multiple_of(local[number] // LANES * LANES, LANES)
        return pltpu.make_async_copy(
            vectors_ref.at[part, :, :, pl.ds(start, LANES)],
            columns_ref.at[number, part],
            sems.at[number, part],
        )

    for number in range(source_count):
        @pl.when(held[number])
        def _(number=number):
            for part in range(parts):
                copy(number, part).start()

    lane = lax.broadcasted_iota(jnp.int32, (8, LANES), 1)
    for number in range(source_count):
        @pl.when(held[number])
        def _(number=number):
            chosen = jnp.where(lane == local[number] % LANES, 1.0, 0.0).astype(jnp.bfloat16)
            for part in range(parts):
                copy(number, part).wait()
                row = lax.dot_general(
                    chosen,
                    columns_ref[number, part].reshape(spin_color * mode_count, LANES),
                    (((1,), (1,)), ((), ())),
                    preferred_element_type=jnp.float32,
                )
                base = (part * source_count + number) * spin_color
                for component in range(spin_color):
                    total_ref[base + component, :] = row[0, component * mode_count:(component + 1) * mode_count]
    values.wait()
    divisor = divisor_ref[...]
    columns = source_count * spin_color
    real, imag = total_ref[:columns, :] / divisor, -total_ref[columns:, :] / divisor
    rows_ref[...] = jnp.concatenate([real, imag], axis=0).astype(rows_ref.dtype)


def pick(source_sites, eigenvalues, vectors):
    parts, spin_color, mode_count, site_count = vectors.shape
    source_count = source_sites.shape[0]
    rows = parts * source_count * spin_color
    return pl.pallas_call(
        pick_kernel,
        out_shape=jax.ShapeDtypeStruct((rows, mode_count), vectors.dtype),
        in_specs=[pl.BlockSpec(memory_space=pl.ANY)] * 3,
        out_specs=pl.BlockSpec(memory_space=pltpu.VMEM),
        scratch_shapes=[
            pltpu.SMEM(source_sites.shape, source_sites.dtype),
            pltpu.VMEM(eigenvalues.shape, eigenvalues.dtype),
            pltpu.VMEM((source_count, parts, spin_color, mode_count, LANES), vectors.dtype),
            pltpu.VMEM((rows, mode_count), jnp.float32),
            pltpu.SemaphoreType.DMA,
            pltpu.SemaphoreType.DMA,
            pltpu.SemaphoreType.DMA((source_count, parts)),
        ],
        compiler_params=pltpu.CompilerParams(vmem_limit_bytes=24 * MIB),
        name="pick",
    )(source_sites, eigenvalues, vectors)


def iota(shape, dim):
    return lax.broadcasted_iota(jnp.int32, shape, dim)


def shares(columns, ways, core, plane):
    share = columns // ways
    shape = (ROWS, 2 * columns)
    row, entry = iota(shape, 0), iota(shape, 1)
    place, inner = row // (2 * share), row % (2 * share)
    its_core = jnp.where(place % 2 == 0, 1 - core, core)
    its_plane = jnp.where((place == 0) | (place == 3), plane, 1 - plane)
    column, part = (2 * its_plane + its_core) * share + inner // 2, inner % 2
    real, imag = (entry == column), (entry == column + columns)
    one = jnp.float32(1)
    zero = jnp.float32(0)
    on_real = jnp.where(part == 0, jnp.where(real, one, zero), jnp.where(imag, one, zero))
    on_imag = jnp.where(part == 0, jnp.where(imag, -one, zero), jnp.where(real, one, zero))
    return on_real.astype(jnp.bfloat16), on_imag.astype(jnp.bfloat16)


def dot(left, right):
    return jnp.dot(left, right, preferred_element_type=jnp.float32)


def multiply(left, vectors_ref, start, sent_ref, kept_ref, flat_ref, share):
    count = flat_ref.shape[1] // share
    for inner in range(count):
        component = start + inner
        product = dot(left[0], vectors_ref[0, component]) + dot(left[1], vectors_ref[1, component])
        for place in range(flat_ref.shape[0]):
            flat_ref[place, pl.ds(inner * share, share), :] = product[place * share:(place + 1) * share]
    sent_ref[...] = flat_ref[:2].astype(sent_ref.dtype)
    kept_ref[...] = flat_ref[2:].astype(kept_ref.dtype)


def first_kernel(rows_ref, vectors_ref, sent_ref, kept_ref, left_ref, flat_ref):
    columns = rows_ref.shape[0] // 2
    ways = flat_ref.shape[0]
    index = lax.axis_index("modes")
    weights = rows_ref[...]
    on_real, on_imag = shares(columns, ways, index % 2, index // 2)
    left = [dot(on, weights).astype(jnp.bfloat16) for on in (on_real, on_imag)]
    left_ref[0] = left[0]
    left_ref[1] = left[1]
    multiply(left, vectors_ref, 0, sent_ref, kept_ref, flat_ref, 2 * columns // ways)


def next_kernel(start, share, left_ref, vectors_ref, sent_ref, kept_ref, flat_ref):
    multiply([left_ref[0], left_ref[1]], vectors_ref, start, sent_ref, kept_ref, flat_ref, share)


def project(rows, vectors, ways):
    parts, spin_color, mode_count, site_count = vectors.shape
    share = rows.shape[0] // ways
    vmem = pl.BlockSpec(memory_space=pltpu.VMEM)

    def call(kernel, operands, count, extra, name):
        shape = (2, count * share, site_count)
        size = 2 * parts * count * mode_count * site_count
        return pl.pallas_call(
            kernel,
            out_shape=[jax.ShapeDtypeStruct(shape, jnp.bfloat16), jax.ShapeDtypeStruct(shape, jnp.float32)] + extra,
            in_specs=[vmem] * len(operands),
            out_specs=[vmem] * (2 + len(extra)),
            scratch_shapes=[pltpu.VMEM((ways, count * share, site_count), jnp.float32)],
            compiler_params=pltpu.CompilerParams(vmem_limit_bytes=24 * MIB),
            cost_estimate=pl.CostEstimate(flops=size * ROWS, bytes_accessed=size, transcendentals=0),
            name=name,
        )(*operands)

    left = jax.ShapeDtypeStruct((2, ROWS, mode_count), jnp.bfloat16)
    *first, left = call(first_kernel, (rows, vectors), STEPS[0], [left], "first")
    results = [first]
    start = STEPS[0]
    for count in STEPS[1:]:
        results.append(call(functools.partial(next_kernel, start, share), (left, vectors), count, [], "rest"))
        start += count
    return results


def swap(block, axis, size, bit):
    return lax.ppermute(block, axis, [(index, index ^ bit) for index in range(size)])


def on_device(eigvecs, eigenvalues, source_sites):
    site_ways, mode_ways = lax.axis_size("sites"), lax.axis_size("modes")
    vectors = jnp.transpose(eigvecs, (0, 2, 1, 3))
    parts, spin_color, mode_count, site_count = vectors.shape
    operands = (source_sites, eigenvalues.reshape(1, mode_count), vectors)
    rows = pick(*[pltpu.with_memory_space_constraint(operand, pltpu.HBM) for operand in operands])
    near = swap(rows, "sites", site_ways, 6)
    far = [swap(rows, "sites", site_ways, bit) for bit in (5, 3)]
    pair = rows + near
    late = [swap(pair, "sites", site_ways, bit) for bit in (1, 2)]
    rows = pair
    for block in far + late:
        rows = rows + block
    bit = 8
    while bit < site_ways:
        rows = rows + swap(rows, "sites", site_ways, bit)
        bit *= 2
    halves = []
    for sent, kept in project(rows, pltpu.with_memory_space_constraint(vectors, pltpu.VMEM), mode_ways):
        got = swap(sent, "modes", mode_ways, 1)
        across = (kept[0] + got[1].astype(jnp.float32)).astype(jnp.bfloat16)
        arrived = swap(across, "modes", mode_ways, 3)
        halves.append(kept[1] + got[0].astype(jnp.float32) + arrived.astype(jnp.float32))
    total = jnp.concatenate(halves, axis=0)
    share = total.shape[0] // spin_color // 2
    return jnp.transpose(total.reshape(spin_color, share, 2, site_count), (1, 2, 0, 3))


def solution(mesh):
    in_specs = (P(None, "modes", None, "sites"), P("modes"), P())
    out_specs = P("modes", None, None, "sites")
    return jax.shard_map(on_device, mesh=mesh, in_specs=in_specs, out_specs=out_specs, check_vma=False)
```
